32 devices in a mesh: grp: 2 (over x), ha: 16 (over z, y, core).
Axes of the slice: x: 2, y: 2, z: 4, core: 2. Of those that a mesh axis runs over, the one named last changes fastest.
Arguments:
- features: bfloat16 [4, 16, 128, 384], P('grp', 'ha'), parts along dimension 0, may hold values from -8 to 8
- first_cache: bfloat16 [4, 16, 128, 384], P('grp', 'ha'), parts along dimension 0, may hold values from -6 to 6
- second_cache: bfloat16 [4, 32, 256, 192], P('grp', 'ha'), parts along dimension 0, may hold values from -6 to 6
- w_query: bfloat16 [384, 384], replicated, may hold values from -2 to 2
- w_key: bfloat16 [384, 384], replicated, may hold values from -2 to 2
- w_value: bfloat16 [384, 384], replicated, may hold values from -0.3125 to 0.3125
- w_output: bfloat16 [384, 384], replicated, may hold values from -0.625 to 0.625
- w_first: bfloat16 [3, 3, 3, 384, 384], replicated, may hold values from -0.0625 to 0.0625
- w_upsample: bfloat16 [3, 3, 384, 192], replicated, may hold values from -0.109375 to 0.109375
- w_second: bfloat16 [3, 3, 3, 192, 192], replicated, may hold values from -0.078125 to 0.078125
Outputs:
- decoded: bfloat16 [4, 32, 256, 192], P('grp', 'ha'), parts along dimension 0
The draws below stay inside these ranges and needn't reach their ends.
There are 2 independent parts, one for each index of `grp`. The reference program is written for one: setup_inputs(seed, part) draws one part's arguments, and reference() takes and returns one part's arrays. A program takes and returns all parts, laid end to end along the dimension named above; an argument that names none is the same for every part. Nothing has to cross between parts.
All inputs are finite; a program needn't handle non-finite values.
Results may differ from the reference program's by a relative error of at most 0.015.
Values may be sent and summed in bfloat16 or wider, within the bound.
A program may use at most 128 MiB of HBM per device.

```python
import math
import jax
import jax.numpy as jnp
from jax import lax

C = 384
C2 = 192
CACHE_T = 2
FRAMES = 2
LAT_W = 128
LAT_H = 16


def query_key_pair(key):
    base = jnp.clip(jax.random.normal(jax.random.fold_in(key, 101), (C, C), jnp.float32), -4.0, 4.0)
    other = jnp.clip(jax.random.normal(jax.random.fold_in(key, 102), (C, C), jnp.float32), -4.0, 4.0)
    spread = math.sqrt(math.log(LAT_H * LAT_W / 8.0))
    sigma = math.sqrt(spread / C)
    first = base * sigma
    second = other * sigma
    return (first, second)


def draw_w_query(key, part):
    return query_key_pair(key)[0].astype(jnp.bfloat16)


def draw_w_key(key, part):
    return query_key_pair(key)[1].astype(jnp.bfloat16)


def draw_features(key, part):
    shape = (FRAMES, LAT_H, LAT_W, C)
    result = jnp.clip(jax.random.normal(jax.random.fold_in(key, 206), shape, jnp.float32), -6.0, 6.0)
    return result.astype(jnp.bfloat16)


def level_of(key, dims, cuts, smallest, top_value):
    def one(position, shards_of):
        steps = jax.random.uniform(jax.random.fold_in(jax.random.fold_in(key, 6), position), (shards_of,), jnp.float32, smallest / len(cuts), top_value / len(cuts))
        return jnp.repeat(jnp.exp(steps), dims[position] // shards_of).reshape((-1,) + (1,) * (len(dims) - position - 1))

    level = one(*cuts[0])
    for cut in cuts[1:]:
        level = level * one(*cut)
    return level


def gaussian(stream_key, dims, scale, limit, pieces=(), kind=jnp.bfloat16):
    level = level_of(stream_key, dims, pieces, -0.22, 0.18) if pieces else 1.0
    values = jax.random.normal(stream_key, dims, jnp.float32) * scale * level
    return jnp.minimum(jnp.maximum(values, -limit), limit).astype(kind)


def setup_inputs(seed: int = 0, part: int = 0) -> dict:
    key_list = jax.random.split(jax.random.key(seed), 11)
    own_keys = jax.random.split(jax.random.fold_in(key_list[10], part), 11)
    features = draw_features(jax.random.fold_in(jax.random.fold_in(key_list[10], part), 71), part)
    first_cache = gaussian(own_keys[1], (CACHE_T, LAT_H, LAT_W, C), 1.0, 6.0, ((1, 16),))
    second_cache = gaussian(own_keys[2], (CACHE_T, 2 * LAT_H, 2 * LAT_W, C2), 1.0, 6.0, ((1, 16),))
    w_query = draw_w_query(jax.random.fold_in(key_list[10], 71), part)
    w_key = draw_w_key(jax.random.fold_in(key_list[10], 71), part)
    w_value = gaussian(key_list[5], (C, C), C ** -0.5, 0.3125)
    w_output = gaussian(key_list[6], (C, C), (C // 4) ** -0.5, 0.625)
    w_first = gaussian(key_list[7], (3, 3, 3, C, C), (27 * C) ** -0.5, 0.0625)
    w_upsample = gaussian(key_list[8], (3, 3, C, C2), (9 * C) ** -0.5, 0.109375)
    w_second = gaussian(key_list[9], (3, 3, 3, C2, C2), (27 * C2) ** -0.5, 0.078125)
    return dict(features=features, first_cache=first_cache, second_cache=second_cache, w_query=w_query, w_key=w_key, w_value=w_value, w_output=w_output, w_first=w_first, w_upsample=w_upsample, w_second=w_second)


def rms_scale(tensor):
    widened = tensor.astype(jnp.float32)
    return widened * lax.rsqrt(lax.optimization_barrier(jnp.mean(widened * widened, axis=-1, keepdims=True)) + 1e-06)

def conv_apply(stacked, weight, time_taps):
    padded = jnp.pad(stacked.astype(jnp.float32), ((0, 0), (1, 1), (1, 1), (0, 0)))
    frames_out = stacked.shape[0] - time_taps + 1
    height_out = stacked.shape[1]
    width_out = stacked.shape[2]
    result = jnp.zeros((frames_out, height_out, width_out, weight.shape[-1]), jnp.float32)
    for time_off in range(time_taps):
        for row_off in range(3):
            for col_off in range(3):
                window = padded[time_off:time_off + frames_out, row_off:row_off + height_out, col_off:col_off + width_out]
                kernel = weight[time_off, row_off, col_off].astype(jnp.float32)
                result = result + jnp.einsum('fhwc,cd->fhwd', window, kernel)
    return result

def attend_frame(queries, keys_all, values_all):
    token_count = queries.shape[0]
    block = math.gcd(token_count, 512)
    score_scale = 1.0 / math.sqrt(queries.shape[1])

    def one_block(query_rows):
        scores = jnp.dot(query_rows, keys_all.T, preferred_element_type=jnp.float32) * score_scale
        largest = lax.optimization_barrier(jnp.max(scores, axis=-1, keepdims=True))
        weights = jnp.exp(scores - largest)
        weight_sum = lax.optimization_barrier(jnp.sum(weights, axis=-1, keepdims=True))
        summed = jnp.dot(weights.astype(jnp.bfloat16), values_all, preferred_element_type=jnp.float32)
        return (summed / weight_sum).astype(jnp.bfloat16)
    blocks = queries.reshape(token_count // block, block, queries.shape[1])
    return lax.map(one_block, blocks).reshape(token_count, queries.shape[1])

def reference(features, first_cache, second_cache, w_query, w_key, w_value, w_output, w_first, w_upsample, w_second):
    frame_count, height, width, channels = features.shape
    normed = rms_scale(features).astype(jnp.bfloat16)
    mixed_frames = []
    for frame in range(frame_count):
        tokens = normed[frame].reshape(height * width, channels)
        queries = jnp.dot(tokens, w_query, preferred_element_type=jnp.float32).astype(jnp.bfloat16)
        keys_all = jnp.dot(tokens, w_key, preferred_element_type=jnp.float32).astype(jnp.bfloat16)
        values_all = jnp.dot(tokens, w_value, preferred_element_type=jnp.float32).astype(jnp.bfloat16)
        attended = attend_frame(queries, keys_all, values_all)
        projected = jnp.dot(attended, w_output, preferred_element_type=jnp.float32)
        mixed_frames.append((features[frame].astype(jnp.float32) + projected.reshape(height, width, channels)).astype(jnp.bfloat16))
    mixed = jnp.stack(mixed_frames, axis=0)
    first_in = jax.nn.silu(rms_scale(mixed)).astype(jnp.bfloat16)
    first_stack = jnp.concatenate([first_cache, first_in], axis=0)
    block_out = (mixed.astype(jnp.float32) + conv_apply(first_stack, w_first, 3)).astype(jnp.bfloat16)
    enlarged = jnp.repeat(jnp.repeat(block_out, 2, axis=1), 2, axis=2)
    upsampled = conv_apply(enlarged, w_upsample[None], 1).astype(jnp.bfloat16)
    second_in = jax.nn.silu(rms_scale(upsampled)).astype(jnp.bfloat16)
    second_stack = jnp.concatenate([second_cache, second_in], axis=0)
    return (upsampled.astype(jnp.float32) + conv_apply(second_stack, w_second, 3)).astype(jnp.bfloat16)
```

```python
import functools
import math

import jax
import jax.numpy as jnp
from jax import lax
from jax.experimental import pallas as pl
from jax.experimental.pallas import tpu as pltpu
from jax.sharding import PartitionSpec as P

F32 = jnp.float32
BF16 = jnp.bfloat16


def dot(a, b):
    return jnp.dot(a, b, preferred_element_type=F32)


def dot_t(a, b):
    return lax.dot_general(a, b, (((1,), (1,)), ((), ())), preferred_element_type=F32)


def rms(v):
    return v * lax.rsqrt(jnp.mean(v * v, axis=-1, keepdims=True) + 1e-06)


def silu(v):
    return v / (1.0 + jnp.exp(-v))


def from_left(v, width):
    at = lax.broadcasted_iota(jnp.int32, v.shape, 0) % width
    return jnp.where(at == 0, 0.0, pltpu.roll(v, 1, 0))


def from_right(v, width):
    at = lax.broadcasted_iota(jnp.int32, v.shape, 0) % width
    return jnp.where(at == width - 1, 0.0, pltpu.roll(v, v.shape[0] - 1, 0))


def kernel(
    n,
    feat, fc, sc, wq, wk, wv, wo, w1_hbm, wu_hbm, w2_hbm,
    out,
    fb, ring, acc, top, total, fs, mx, bo, ss, up, c1, c2, w1, wu, w2,
    l_sem, e0_s, e0_r, g_s, g_r, h_s, h_r, e1_s, e1_r, e2_s, e2_r,
):
    width, chan = feat.shape[1], feat.shape[2]
    chan2 = w2.shape[-1]
    chips = n // 2
    half = chips // 2
    me = lax.axis_index("ha")
    core, chip = me % 2, me // 2
    other = 1 - core
    zz, yy = chip // 2, chip % 2
    place = zz + yy * (2 * half - 1 - 2 * zz)

    def at_place(p):
        side = p // half
        level = p + side * (2 * half - 1 - 2 * p)
        return (level * 2 + side) * 2 + core

    nxt = at_place((place + 1) % chips)
    prv = at_place((place + chips - 1) % chips)
    partner = chip * 2 + other
    first, last = me == 0, me == n - 1
    low, high = chip > 0, chip < chips - 1

    def copy(src, dst, ssem, rsem, dev):
        return pltpu.make_async_remote_copy(
            src_ref=src, dst_ref=dst, send_sem=ssem, recv_sem=rsem,
            device_id={"ha": dev}, device_id_type=pl.DeviceIdType.MESH,
        )

    loads = [
        pltpu.make_async_copy(src, dst, l_sem.at[k])
        for k, (src, dst) in enumerate(((w1_hbm, w1), (w2_hbm, w2), (wu_hbm, wu)))
    ]
    for load in loads:
        load.start()

    barrier = pltpu.get_barrier_semaphore()

    def greet(dev):
        pl.semaphore_signal(
            barrier, inc=1, device_id={"ha": dev}, device_id_type=pl.DeviceIdType.MESH
        )

    greet(partner)
    greet(nxt)
    greet(prv)

    @pl.when(jnp.logical_and(core == 0, low))
    def _():
        greet(2 * chip - 2)
        greet(2 * chip - 1)

    @pl.when(jnp.logical_and(core == 1, high))
    def _():
        greet(2 * chip + 2)
        greet(2 * chip + 3)

    pl.semaphore_wait(barrier, 3 + low.astype(jnp.int32) + high.astype(jnp.int32))

    swap = copy(feat.at[other], fb.at[core], e0_s.at[0], e0_r.at[0], partner)
    swap.start()

    def ring_copy(src_slot, slot, row, dev):
        return copy(
            ring.at[src_slot, row], ring.at[slot, row], g_s.at[slot, row], g_r.at[slot, row], dev
        )

    fb[core] = feat[core]
    ring[0, core] = rms(feat[core].astype(F32)).astype(BF16)
    ring_copy(0, 1, core, nxt).start()
    ring_copy(0, chips - 1, core, prv).start()
    copy(feat.at[core], fb.at[other], e0_s.at[0], e0_r.at[0], partner).wait_recv()
    ring[0, other] = rms(fb[other].astype(F32)).astype(BF16)
    ring_copy(0, 1, other, nxt).start()
    ring_copy(0, chips - 1, other, prv).start()

    fc_up = copy(fc, fs.at[pl.ds(0, 2), 0], h_s.at[0], h_r.at[0], me + 1)
    fc_down = copy(fc, fs.at[pl.ds(0, 2), 2], h_s.at[1], h_r.at[1], me - 1)
    sc_up = copy(sc.at[1], ss.at[0, :, pl.ds(0, 2)], h_s.at[2], h_r.at[2], me + 1)
    sc_down = copy(sc.at[0], ss.at[3, :, pl.ds(0, 2)], h_s.at[3], h_r.at[3], me - 1)

    @pl.when(jnp.logical_not(last))
    def _():
        fc_up.start()
        sc_up.start()

    @pl.when(jnp.logical_not(first))
    def _():
        fc_down.start()
        sc_down.start()

    fs[0:2, 1] = fc[...]
    ss[1, :, 0:2] = sc[0]
    ss[2, :, 0:2] = sc[1]

    @pl.when(first)
    def _():
        fs[:, 0] = jnp.zeros((4, width, chan), BF16)
        ss[0, :, 0:2] = jnp.zeros((2, 2, width, chan2), BF16)
        bo[0] = jnp.zeros((2, width, chan), BF16)

    @pl.when(last)
    def _():
        fs[:, 2] = jnp.zeros((4, width, chan), BF16)
        ss[3, :, 0:2] = jnp.zeros((2, 2, width, chan2), BF16)
        bo[2] = jnp.zeros((2, width, chan), BF16)

    own = ring[0].reshape(2 * width, chan)
    queries = dot(own, wq[...]).astype(BF16)
    queries = (dot_t(queries, wk[...]) * (1.0 / math.sqrt(chan))).astype(BF16)

    def scores_of(slot):
        return dot_t(queries, ring[slot].reshape(2 * width, chan))

    scores = scores_of(0)
    largest = jnp.max(scores, axis=-1, keepdims=True)
    weights = jnp.exp(scores - largest)
    top[...] = largest
    total[...] = jnp.sum(weights, axis=-1, keepdims=True)
    acc[...] = dot(weights.astype(BF16), own)

    def attend(slots):
        parts = [scores_of(slot) for slot in slots]
        before = top[...]
        largest = before
        for part in parts:
            largest = jnp.maximum(largest, jnp.max(part, axis=-1, keepdims=True))
        shrink = jnp.exp(before - largest)
        sums, mixed_in = total[...] * shrink, acc[...] * shrink
        for slot, part in zip(slots, parts):
            weights = jnp.exp(part - largest)
            sums += jnp.sum(weights, axis=-1, keepdims=True)
            mixed_in += dot(weights.astype(BF16), ring[slot].reshape(2 * width, chan))
        top[...] = largest
        total[...] = sums
        acc[...] = mixed_in

    for step in range(1, half):
        for row in (core, other):
            ring_copy(step, step, row, nxt).wait_recv()
            if step + 1 < half:
                ring_copy(step, step + 1, row, nxt).start()
            else:
                pl.when(row == 0)(ring_copy(step, step + 1, 0, nxt).start)
            ring_copy(chips - step, chips - step, row, prv).wait_recv()
            if step + 1 < half:
                ring_copy(chips - step, chips - step - 1, row, prv).start()
            else:
                pl.when(row == 1)(ring_copy(chips - step, chips - step - 1, 1, prv).start)
        attend((step, chips - step))

    @pl.when(jnp.logical_not(first))
    def _():
        fc_up.wait_recv()
        sc_up.wait_recv()

    @pl.when(jnp.logical_not(last))
    def _():
        fc_down.wait_recv()
        sc_down.wait_recv()

    for load in loads:
        load.wait()

    def first_conv(times):
        totals = [None] * 3
        for a in times:
            for b in range(3):
                rows = fs[a : a + 2, b].reshape(2 * width, chan)
                for c in range(3):
                    term = dot(rows, w1[a, b, c])
                    totals[c] = term if totals[c] is None else totals[c] + term
        return totals

    def second_conv(times, k):
        taps = (((0, 1), (1, 2)), ((0, 0), (1, 1)), ((1, 0),), ((0, 2),))[k]
        sums = None
        for a in times:
            for b in range(3):
                for parity, c in taps:
                    rows = ss[b : b + 2, parity, a : a + 2].reshape(4 * width, chan2)
                    term = dot(rows, w2[a, b, c])
                    sums = term if sums is None else sums + term
        return sums

    for c, part in enumerate(first_conv((0,))):
        c1[c] = part
    for k in range(4):
        c2[k] = second_conv((0,), k)

    ring_copy(half, half, 0, nxt).wait_recv()
    ring_copy(half, half, 1, prv).wait_recv()
    attend((half,))

    attended = dot((acc[...] / total[...]).astype(BF16), wv[...])
    projected = dot(attended.astype(BF16), wo[...])
    mixed = (fb[...].reshape(2 * width, chan).astype(F32) + projected).astype(BF16)
    entering = silu(rms(mixed.astype(F32))).astype(BF16).reshape(2, width, chan)
    mixed = mixed.reshape(2, width, chan)
    mine = 2 + core
    fs[mine, pl.ds(other, 2)] = entering
    mx[0] = mixed[0]
    mx[1] = mixed[1]

    to_partner = copy(
        fs.at[mine, pl.ds(other, 2)], fs.at[mine, pl.ds(core, 2)], e1_s.at[0], e1_r.at[0], partner
    )
    mix_partner = copy(mx.at[other], mx.at[2], e1_s.at[1], e1_r.at[1], partner)
    row_up = copy(
        fs.at[mine, other + 1], fs.at[mine, 0], e1_s.at[2], e1_r.at[2 + core], 2 * chip + 2
    )
    row_down = copy(
        fs.at[mine, other], fs.at[mine, 2], e1_s.at[3], e1_r.at[2 + core], 2 * chip - 1
    )
    pl.when(high)(row_up.start)
    pl.when(low)(row_down.start)
    to_partner.start()
    mix_partner.start()

    theirs = 2 + other
    copy(
        fs.at[theirs, pl.ds(core, 2)], fs.at[theirs, pl.ds(other, 2)],
        e1_s.at[0], e1_r.at[0], partner,
    ).wait_recv()
    mix_partner.wait_recv()

    @pl.when(jnp.logical_and(core == 0, low))
    def _():
        for f in range(2):
            copy(
                fs.at[2 + f, 1], fs.at[2 + f, 0], e1_s.at[2], e1_r.at[2 + f], 2 * chip - 2 + f
            ).wait_recv()

    @pl.when(jnp.logical_and(core == 1, high))
    def _():
        for f in range(2):
            copy(
                fs.at[2 + f, 1], fs.at[2 + f, 2], e1_s.at[3], e1_r.at[2 + f], 2 * chip + 2 + f
            ).wait_recv()

    sums = [c1[c] + part for c, part in enumerate(first_conv((1, 2)))]
    block = from_left(sums[0], width) + sums[1] + from_right(sums[2], width)
    block = block.reshape(2, width, chan)
    bo[1, core] = (mx[core].astype(F32) + jnp.where(core == 0, block[0], block[1])).astype(BF16)
    bo[1, other] = (mx[2].astype(F32) + jnp.where(core == 0, block[1], block[0])).astype(BF16)

    bo_up = copy(bo.at[1], bo.at[0], e2_s.at[0], e2_r.at[0], me + 1)
    bo_down = copy(bo.at[1], bo.at[2], e2_s.at[1], e2_r.at[1], me - 1)
    pl.when(jnp.logical_not(last))(bo_up.start)
    pl.when(jnp.logical_not(first))(bo_down.start)

    here = bo[1].reshape(2 * width, chan)
    y = [[dot(here, wu[b, c]) for c in range(3)] for b in range(3)]
    rows = [
        [y[2][c] for c in range(3)],
        [y[1][c] + y[2][c] for c in range(3)],
        [y[0][c] + y[1][c] for c in range(3)],
        [y[0][c] for c in range(3)],
    ]
    pl.when(jnp.logical_not(first))(bo_up.wait_recv)
    pl.when(jnp.logical_not(last))(bo_down.wait_recv)
    above = bo[0].reshape(2 * width, chan)
    below = bo[2].reshape(2 * width, chan)
    for c in range(3):
        near, far = dot(above, wu[0, c]), dot(above, wu[1, c])
        rows[0][c] += near + far
        rows[1][c] += near
        near, far = dot(below, wu[2, c]), dot(below, wu[1, c])
        rows[2][c] += near
        rows[3][c] += near + far
    for u in range(4):
        left, middle, right = rows[u]
        phases = (
            from_left(left, width) + middle + right,
            left + middle + from_right(right, width),
        )
        for parity, value in enumerate(phases):
            value = value.astype(BF16)
            if u in (1, 2):
                up[u - 1, parity] = value.reshape(2, width, chan2)
            entering = silu(rms(value.astype(F32)))
            if u == 0:
                entering = jnp.where(first, 0.0, entering)
            if u == 3:
                entering = jnp.where(last, 0.0, entering)
            ss[u, parity, 2:4] = entering.astype(BF16).reshape(2, width, chan2)

    late = (1, 2)
    even = c2[0] + second_conv(late, 0) + from_left(c2[2] + second_conv(late, 2), width)
    out[:, 0] = (up[:, 0].astype(F32) + even.reshape(2, 2, width, chan2)).astype(BF16)
    odd = c2[1] + second_conv(late, 1) + from_right(c2[3] + second_conv(late, 3), width)
    out[:, 1] = (up[:, 1].astype(F32) + odd.reshape(2, 2, width, chan2)).astype(BF16)

    swap.wait_send()
    for slot in range(1, chips):
        for row in range(2):
            ring_copy(slot, slot, row, nxt).wait_send()

    @pl.when(jnp.logical_not(last))
    def _():
        fc_up.wait_send()
        sc_up.wait_send()
        bo_up.wait_send()

    @pl.when(jnp.logical_not(first))
    def _():
        fc_down.wait_send()
        sc_down.wait_send()
        bo_down.wait_send()

    pl.when(high)(row_up.wait_send)
    pl.when(low)(row_down.wait_send)
    to_partner.wait_send()
    mix_partner.wait_send()


def per_device(features, first_cache, second_cache, wq, wk, wv, wo, w1, wu, w2):
    n = lax.axis_size("ha")
    width, chan = features.shape[2:]
    chan2 = w2.shape[-1]
    chips = n // 2
    feat = features.reshape(2, width, chan)
    fc = first_cache.reshape(2, width, chan)
    sc = second_cache.reshape(2, 2, width, 2, chan2).transpose(1, 3, 0, 2, 4)
    vmem = pl.BlockSpec(memory_space=pltpu.VMEM)
    hbm = pl.BlockSpec(memory_space=pl.ANY)
    dma = pltpu.SemaphoreType.DMA
    out = pl.pallas_call(
        functools.partial(kernel, n),
        out_shape=jax.ShapeDtypeStruct((2, 2, 2, width, chan2), BF16),
        in_specs=[vmem] * 7 + [hbm] * 3,
        out_specs=vmem,
        scratch_shapes=[
            pltpu.VMEM((2, width, chan), BF16),
            pltpu.VMEM((chips, 2, width, chan), BF16),
            pltpu.VMEM((2 * width, chan), F32),
            pltpu.VMEM((2 * width, 1), F32),
            pltpu.VMEM((2 * width, 1), F32),
            pltpu.VMEM((4, 3, width, chan), BF16),
            pltpu.VMEM((3, width, chan), BF16),
            pltpu.VMEM((3, 2, width, chan), BF16),
            pltpu.VMEM((4, 2, 4, width, chan2), BF16),
            pltpu.VMEM((2, 2, 2, width, chan2), BF16),
            pltpu.VMEM((3, 2 * width, chan), F32),
            pltpu.VMEM((4, 4 * width, chan2), F32),
            pltpu.VMEM(w1.shape, BF16),
            pltpu.VMEM(wu.shape, BF16),
            pltpu.VMEM(w2.shape, BF16),
            dma((3,)),
            dma((1,)),
            dma((1,)),
            dma((chips, 2)),
            dma((chips, 2)),
            dma((4,)),
            dma((4,)),
            dma((4,)),
            dma((4,)),
            dma((2,)),
            dma((2,)),
        ],
        compiler_params=pltpu.CompilerParams(
            collective_id=0, has_side_effects=True, vmem_limit_bytes=56 * 2**20
        ),
        name="decoder_window",
    )(feat, fc, sc, wq, wk, wv, wo, w1, wu, w2)
    return out.transpose(2, 0, 3, 1, 4).reshape(2, 2, 2 * width, chan2)


def solution(mesh):
    split = P("grp", "ha", None, None)
    return jax.shard_map(
        per_device,
        mesh=mesh,
        in_specs=(split,) * 3 + (P(),) * 7,
        out_specs=split,
        check_vma=False,
    )
```

```python
import functools
import math

import jax
import jax.numpy as jnp
from jax import lax
from jax.experimental import pallas as pl
from jax.experimental.pallas import tpu as pltpu
from jax.sharding import PartitionSpec as P

F32 = jnp.float32
BF16 = jnp.bfloat16


def dot(a, b):
    return jnp.dot(a, b, preferred_element_type=F32)


def dot_t(a, b):
    return lax.dot_general(a, b, (((1,), (1,)), ((), ())), preferred_element_type=F32)


def rms(v):
    return v * lax.rsqrt(jnp.mean(v * v, axis=-1, keepdims=True) + 1e-06)


def silu(v):
    return v * (0.5 + 0.5 * jnp.tanh(0.5 * v))


def from_left(v, width):
    at = lax.broadcasted_iota(jnp.int32, v.shape, 0) % width
    return jnp.where(at == 0, 0.0, pltpu.roll(v, 1, 0))


def from_right(v, width):
    at = lax.broadcasted_iota(jnp.int32, v.shape, 0) % width
    return jnp.where(at == width - 1, 0.0, pltpu.roll(v, v.shape[0] - 1, 0))


def kernel(
    n,
    feat, fc, sc, wq_hbm, wk_hbm, wv_hbm, wo_hbm, w1_hbm, wu_hbm, w2_hbm,
    out,
    fb, ring, acc, top, total, fs, mx, bo, ss, up, c1, c2,
    wq, wk, wv, wo, w1, wu, w2, wu_turned,
    l_sem, e0_s, e0_r, g_s, g_r, h_s, h_r, e1_s, e1_r, e2_s, e2_r,
):
    width, chan = feat.shape[1], feat.shape[2]
    chan2 = w2.shape[-1]
    chips = n // 2
    half = chips // 2
    me = lax.axis_index("ha")
    core, chip = me % 2, me // 2
    other = 1 - core
    zz, yy = chip // 2, chip % 2
    place = zz + yy * (2 * half - 1 - 2 * zz)

    def at_place(p):
        side = p // half
        level = p + side * (2 * half - 1 - 2 * p)
        return (level * 2 + side) * 2 + core

    nxt = at_place((place + 1) % chips)
    prv = at_place((place + chips - 1) % chips)
    partner = chip * 2 + other
    first, last = me == 0, me == n - 1
    low, high = chip > 0, chip < chips - 1

    def copy(src, dst, ssem, rsem, dev):
        return pltpu.make_async_remote_copy(
            src_ref=src, dst_ref=dst, send_sem=ssem, recv_sem=rsem,
            device_id={"ha": dev}, device_id_type=pl.DeviceIdType.MESH,
        )

    loads = [
        pltpu.make_async_copy(src, dst, l_sem.at[k])
        for k, (src, dst) in enumerate(
            (
                (wq_hbm, wq), (wk_hbm, wk), (wu_hbm, wu_turned), (w1_hbm, w1),
                (w2_hbm, w2), (wv_hbm, wv), (wo_hbm, wo),
            )
        )
    ]

    barrier = pltpu.get_barrier_semaphore()

    def greet(dev):
        pl.semaphore_signal(
            barrier, inc=1, device_id={"ha": dev}, device_id_type=pl.DeviceIdType.MESH
        )

    greet(partner)
    greet(nxt)
    greet(prv)

    @pl.when(jnp.logical_and(core == 0, low))
    def _():
        greet(2 * chip - 2)
        greet(2 * chip - 1)

    @pl.when(jnp.logical_and(core == 1, high))
    def _():
        greet(2 * chip + 2)
        greet(2 * chip + 3)

    for load in loads:
        load.start()

    pl.semaphore_wait(barrier, 3 + low.astype(jnp.int32) + high.astype(jnp.int32))

    swap = copy(feat.at[other], fb.at[core], e0_s.at[0], e0_r.at[0], partner)
    swap.start()

    def ring_copy(src_slot, slot, row, dev):
        return copy(
            ring.at[src_slot, row], ring.at[slot, row], g_s.at[slot, row], g_r.at[slot, row], dev
        )

    fb[core] = feat[core]
    ring[0, core] = rms(feat[core].astype(F32)).astype(BF16)
    ring_copy(0, 1, core, nxt).start()
    ring_copy(0, chips - 1, core, prv).start()
    copy(feat.at[core], fb.at[other], e0_s.at[0], e0_r.at[0], partner).wait_recv()
    ring[0, other] = rms(fb[other].astype(F32)).astype(BF16)
    ring_copy(0, 1, other, nxt).start()
    ring_copy(0, chips - 1, other, prv).start()

    for parity in range(2):
        pick = (
            lax.broadcasted_iota(jnp.int32, (width, 2 * width), 1)
            == 2 * lax.broadcasted_iota(jnp.int32, (width, 2 * width), 0) + parity
        ).astype(BF16)
        for f in range(2):
            for r in range(2):
                ss[1 + r, parity, f] = dot_t(pick, sc[f, r]).astype(BF16)

    fc_up = copy(fc, fs.at[pl.ds(0, 2), 0], h_s.at[0], h_r.at[0], me + 1)
    fc_down = copy(fc, fs.at[pl.ds(0, 2), 2], h_s.at[1], h_r.at[1], me - 1)
    sc_up = copy(ss.at[2, :, pl.ds(0, 2)], ss.at[0, :, pl.ds(0, 2)], h_s.at[2], h_r.at[2], me + 1)
    sc_down = copy(ss.at[1, :, pl.ds(0, 2)], ss.at[3, :, pl.ds(0, 2)], h_s.at[3], h_r.at[3], me - 1)

    @pl.when(jnp.logical_not(last))
    def _():
        fc_up.start()
        sc_up.start()

    @pl.when(jnp.logical_not(first))
    def _():
        fc_down.start()
        sc_down.start()

    fs[0:2, 1] = fc[...]

    @pl.when(first)
    def _():
        fs[:, 0] = jnp.zeros((4, width, chan), BF16)
        ss[0, :, 0:2] = jnp.zeros((2, 2, width, chan2), BF16)
        bo[0] = jnp.zeros((2, width, chan), BF16)

    @pl.when(last)
    def _():
        fs[:, 2] = jnp.zeros((4, width, chan), BF16)
        ss[3, :, 0:2] = jnp.zeros((2, 2, width, chan2), BF16)
        bo[2] = jnp.zeros((2, width, chan), BF16)

    loads[0].wait()
    loads[1].wait()
    own = ring[0].reshape(2 * width, chan)
    queries = dot(own, wq[...]).astype(BF16)
    queries = (dot_t(queries, wk[...]) * (1.0 / math.sqrt(chan))).astype(BF16)

    def scores_of(slot):
        return dot_t(queries, ring[slot].reshape(2 * width, chan))

    scores = scores_of(0)
    largest = jnp.max(scores, axis=-1, keepdims=True)
    weights = jnp.exp(scores - largest)
    top[...] = largest
    total[...] = jnp.sum(weights, axis=-1, keepdims=True)
    acc[...] = dot(weights.astype(BF16), own)

    def attend(slots):
        parts = [scores_of(slot) for slot in slots]
        before = top[...]
        largest = before
        for part in parts:
            largest = jnp.maximum(largest, jnp.max(part, axis=-1, keepdims=True))
        shrink = jnp.exp(before - largest)
        sums, mixed_in = total[...] * shrink, acc[...] * shrink
        for slot, part in zip(slots, parts):
            weights = jnp.exp(part - largest)
            sums += jnp.sum(weights, axis=-1, keepdims=True)
            mixed_in += dot(weights.astype(BF16), ring[slot].reshape(2 * width, chan))
        top[...] = largest
        total[...] = sums
        acc[...] = mixed_in

    for step in range(1, half):
        for row in (core, other):
            ring_copy(step, step, row, nxt).wait_recv()
            if step + 1 < half:
                ring_copy(step, step + 1, row, nxt).start()
            else:
                pl.when(row == 0)(ring_copy(step, step + 1, 0, nxt).start)
            ring_copy(chips - step, chips - step, row, prv).wait_recv()
            if step + 1 < half:
                ring_copy(chips - step, chips - step - 1, row, prv).start()
            else:
                pl.when(row == 1)(ring_copy(chips - step, chips - step - 1, 1, prv).start)
        attend((step, chips - step))

    @pl.when(jnp.logical_not(first))
    def _():
        fc_up.wait_recv()
        sc_up.wait_recv()

    @pl.when(jnp.logical_not(last))
    def _():
        fc_down.wait_recv()
        sc_down.wait_recv()

    for load in loads[2:]:
        load.wait()

    def first_conv(a, t, c):
        frames = len(t)
        sums = None
        for b in range(3):
            rows = fs[a + t[0] : a + t[0] + frames, b].reshape(frames * width, chan)
            term = dot(rows, w1[a, b, c])
            sums = term if sums is None else sums + term
        return sums

    def second_conv(a, t, k):
        taps = (((0, 1), (1, 2)), ((0, 0), (1, 1)), ((1, 0),), ((0, 2),))[k]
        frames = len(t)
        sums = None
        for b in range(3):
            for parity, c in taps:
                rows = ss[b : b + 2, parity, a + t[0] : a + t[0] + frames]
                term = dot(rows.reshape(2 * frames * width, chan2), w2[a, b, c])
                sums = term if sums is None else sums + term
        return sums.reshape(2, frames, width, chan2)

    both = (0, 1)
    for c in range(3):
        c1[c] = first_conv(0, both, c)
        c1[c, :width] += first_conv(1, (0,), c)
    for k in range(4):
        c2[k] = second_conv(0, both, k)
        c2[k, :, 0:1] += second_conv(1, (0,), k)
    for b in range(3):
        for c in range(3):
            wu[b, c] = wu_turned[b, c].T

    ring_copy(half, half, 0, nxt).wait_recv()
    ring_copy(half, half, 1, prv).wait_recv()
    attend((half,))

    attended = dot((acc[...] / total[...]).astype(BF16), wv[...])
    projected = dot(attended.astype(BF16), wo[...])
    mixed = (fb[...].reshape(2 * width, chan).astype(F32) + projected).astype(BF16)
    entering = silu(rms(mixed.astype(F32))).astype(BF16).reshape(2, width, chan)
    mixed = mixed.reshape(2, width, chan)
    mine = 2 + core
    fs[mine, pl.ds(other, 2)] = entering
    mx[0] = mixed[0]
    mx[1] = mixed[1]

    to_partner = copy(
        fs.at[mine, pl.ds(other, 2)], fs.at[mine, pl.ds(core, 2)], e1_s.at[0], e1_r.at[0], partner
    )
    mix_partner = copy(mx.at[other], mx.at[2], e1_s.at[1], e1_r.at[1], partner)
    row_up = copy(
        fs.at[mine, other + 1], fs.at[mine, 0], e1_s.at[2], e1_r.at[2 + core], 2 * chip + 2
    )
    row_down = copy(
        fs.at[mine, other], fs.at[mine, 2], e1_s.at[3], e1_r.at[2 + core], 2 * chip - 1
    )
    pl.when(high)(row_up.start)
    pl.when(low)(row_down.start)
    to_partner.start()
    mix_partner.start()

    theirs = 2 + other
    copy(
        fs.at[theirs, pl.ds(core, 2)], fs.at[theirs, pl.ds(other, 2)],
        e1_s.at[0], e1_r.at[0], partner,
    ).wait_recv()
    mix_partner.wait_recv()

    @pl.when(jnp.logical_and(core == 0, low))
    def _():
        for f in range(2):
            copy(
                fs.at[2 + f, 1], fs.at[2 + f, 0], e1_s.at[2], e1_r.at[2 + f], 2 * chip - 2 + f
            ).wait_recv()

    @pl.when(jnp.logical_and(core == 1, high))
    def _():
        for f in range(2):
            copy(
                fs.at[2 + f, 1], fs.at[2 + f, 2], e1_s.at[3], e1_r.at[2 + f], 2 * chip + 2 + f
            ).wait_recv()

    for c in range(3):
        c1[c, width:] += first_conv(1, (1,), c)
    sums = [c1[c] + first_conv(2, both, c) for c in range(3)]
    block = from_left(sums[0], width) + sums[1] + from_right(sums[2], width)
    block = block.reshape(2, width, chan)
    bo[1, core] = (mx[core].astype(F32) + jnp.where(core == 0, block[0], block[1])).astype(BF16)
    bo[1, other] = (mx[2].astype(F32) + jnp.where(core == 0, block[1], block[0])).astype(BF16)

    bo_up = copy(bo.at[1], bo.at[0], e2_s.at[0], e2_r.at[0], me + 1)
    bo_down = copy(bo.at[1], bo.at[2], e2_s.at[1], e2_r.at[1], me - 1)
    pl.when(jnp.logical_not(last))(bo_up.start)
    pl.when(jnp.logical_not(first))(bo_down.start)

    here = bo[1].reshape(2 * width, chan)
    y = [[dot(here, wu[b, c]) for c in range(3)] for b in range(3)]
    rows = [
        [y[2][c] for c in range(3)],
        [y[1][c] + y[2][c] for c in range(3)],
        [y[0][c] + y[1][c] for c in range(3)],
        [y[0][c] for c in range(3)],
    ]
    pl.when(jnp.logical_not(first))(bo_up.wait_recv)
    pl.when(jnp.logical_not(last))(bo_down.wait_recv)
    above = bo[0].reshape(2 * width, chan)
    below = bo[2].reshape(2 * width, chan)
    for c in range(3):
        near, far = dot(above, wu[0, c]), dot(above, wu[1, c])
        rows[0][c] += near + far
        rows[1][c] += near
        near, far = dot(below, wu[2, c]), dot(below, wu[1, c])
        rows[2][c] += near
        rows[3][c] += near + far
    for u in range(4):
        left, middle, right = rows[u]
        phases = (
            from_left(left, width) + middle + right,
            left + middle + from_right(right, width),
        )
        for parity, value in enumerate(phases):
            value = value.astype(BF16)
            if u in (1, 2):
                up[u - 1, parity] = value.reshape(2, width, chan2)
            entering = silu(rms(value.astype(F32)))
            if u == 0:
                entering = jnp.where(first, 0.0, entering)
            if u == 3:
                entering = jnp.where(last, 0.0, entering)
            ss[u, parity, 2:4] = entering.astype(BF16).reshape(2, width, chan2)

    for k in range(4):
        c2[k, :, 1:2] += second_conv(1, (1,), k)

    def final(k):
        return (c2[k] + second_conv(2, both, k)).reshape(4 * width, chan2)

    even = final(0) + from_left(final(2), width)
    odd = final(1) + from_right(final(3), width)
    even, odd = (
        (up[:, parity].astype(F32) + value.reshape(2, 2, width, chan2)).astype(BF16)
        for parity, value in enumerate((even, odd))
    )
    at = lax.broadcasted_iota(jnp.int32, (2 * width, 2 * width), 0)
    column = lax.broadcasted_iota(jnp.int32, (2 * width, 2 * width), 1)
    place_at = (column == jnp.where(at < width, 2 * at, 2 * at - 2 * width + 1)).astype(BF16)
    for f in range(2):
        for r in range(2):
            pair = jnp.concatenate([even[r, f], odd[r, f]], axis=0)
            out[f, r] = lax.dot_general(
                pair, place_at, (((0,), (0,)), ((), ())), preferred_element_type=F32
            ).astype(BF16)

    swap.wait_send()
    for slot in range(1, chips):
        for row in range(2):
            ring_copy(slot, slot, row, nxt).wait_send()

    @pl.when(jnp.logical_not(last))
    def _():
        fc_up.wait_send()
        sc_up.wait_send()
        bo_up.wait_send()

    @pl.when(jnp.logical_not(first))
    def _():
        fc_down.wait_send()
        sc_down.wait_send()
        bo_down.wait_send()

    pl.when(high)(row_up.wait_send)
    pl.when(low)(row_down.wait_send)
    to_partner.wait_send()
    mix_partner.wait_send()


def per_device(features, first_cache, second_cache, wq, wk, wv, wo, w1, wu, w2):
    n = lax.axis_size("ha")
    width, chan = features.shape[2:]
    chan2 = w2.shape[-1]
    chips = n // 2
    feat = features.reshape(2, width, chan)
    fc = first_cache.reshape(2, width, chan)
    sc = second_cache.transpose(0, 1, 3, 2)
    wu = wu.transpose(0, 1, 3, 2)
    vmem = pl.BlockSpec(memory_space=pltpu.VMEM)
    hbm = pl.BlockSpec(memory_space=pl.ANY)
    dma = pltpu.SemaphoreType.DMA
    out = pl.pallas_call(
        functools.partial(kernel, n),
        out_shape=jax.ShapeDtypeStruct((2, 2, chan2, 2 * width), BF16),
        in_specs=[vmem] * 3 + [hbm] * 7,
        out_specs=vmem,
        scratch_shapes=[
            pltpu.VMEM((2, width, chan), BF16),
            pltpu.VMEM((chips, 2, width, chan), BF16),
            pltpu.VMEM((2 * width, chan), F32),
            pltpu.VMEM((2 * width, 1), F32),
            pltpu.VMEM((2 * width, 1), F32),
            pltpu.VMEM((4, 3, width, chan), BF16),
            pltpu.VMEM((3, width, chan), BF16),
            pltpu.VMEM((3, 2, width, chan), BF16),
            pltpu.VMEM((4, 2, 4, width, chan2), BF16),
            pltpu.VMEM((2, 2, 2, width, chan2), BF16),
            pltpu.VMEM((3, 2 * width, chan), F32),
            pltpu.VMEM((4, 2, 2, width, chan2), F32),
            pltpu.VMEM((chan, chan), BF16),
            pltpu.VMEM((chan, chan), BF16),
            pltpu.VMEM((chan, chan), BF16),
            pltpu.VMEM((chan, chan), BF16),
            pltpu.VMEM(w1.shape, BF16),
            pltpu.VMEM((3, 3, chan, chan2), BF16),
            pltpu.VMEM(w2.shape, BF16),
            pltpu.VMEM(wu.shape, BF16),
            dma((7,)),
            dma((1,)),
            dma((1,)),
            dma((chips, 2)),
            dma((chips, 2)),
            dma((4,)),
            dma((4,)),
            dma((4,)),
            dma((4,)),
            dma((2,)),
            dma((2,)),
        ],
        compiler_params=pltpu.CompilerParams(
            collective_id=0, has_side_effects=True, vmem_limit_bytes=56 * 2**20
        ),
        name="decoder_window",
    )(feat, fc, sc, wq, wk, wv, wo, w1, wu, w2)
    return out.transpose(0, 1, 3, 2)


def solution(mesh):
    split = P("grp", "ha", None, None)
    return jax.shard_map(
        per_device,
        mesh=mesh,
        in_specs=(split,) * 3 + (P(),) * 7,
        out_specs=split,
        check_vma=False,
    )
```

```python
import functools
import math

import jax
import jax.numpy as jnp
from jax import lax
from jax.experimental import pallas as pl
from jax.experimental.pallas import tpu as pltpu
from jax.sharding import PartitionSpec as P

F32 = jnp.float32
BF16 = jnp.bfloat16


def dot(a, b):
    return jnp.dot(a, b, preferred_element_type=F32)


def dot_t(a, b):
    return lax.dot_general(a, b, (((1,), (1,)), ((), ())), preferred_element_type=F32)


def rms(v):
    return v * lax.rsqrt(jnp.mean(v * v, axis=-1, keepdims=True) + 1e-06)


def silu(v):
    return v * (0.5 + 0.5 * jnp.tanh(0.5 * v))


def from_left(v, width):
    at = lax.broadcasted_iota(jnp.int32, v.shape, 0) % width
    return jnp.where(at == 0, 0.0, pltpu.roll(v, 1, 0))


def from_right(v, width):
    at = lax.broadcasted_iota(jnp.int32, v.shape, 0) % width
    return jnp.where(at == width - 1, 0.0, pltpu.roll(v, v.shape[0] - 1, 0))


def kernel(
    n,
    feat, fc, sc, wq_hbm, wk_hbm, wv_hbm, wo_hbm, w1_hbm, wu_hbm, w2_hbm,
    out_0, out_1,
    fb, ring, acc, top, total, fs, mx, bo, ss, up, c1, c2,
    wq, wk, wv, wo, w1, wu, w2, wu_turned,
    l_sem, e0_s, e0_r, g_s, g_r, h_s, h_r, e1_s, e1_r, e2_s, e2_r,
):
    width, chan = feat.shape[1], feat.shape[2]
    chan2 = w2.shape[-1]
    chips = n // 2
    half = chips // 2
    me = lax.axis_index("ha")
    core, chip = me % 2, me // 2
    other = 1 - core
    zz, yy = chip // 2, chip % 2
    place = zz + yy * (2 * half - 1 - 2 * zz)

    def at_place(p):
        side = p // half
        level = p + side * (2 * half - 1 - 2 * p)
        return (level * 2 + side) * 2 + core

    nxt = at_place((place + 1) % chips)
    prv = at_place((place + chips - 1) % chips)
    partner = chip * 2 + other
    first, last = me == 0, me == n - 1
    low, high = chip > 0, chip < chips - 1

    def copy(src, dst, ssem, rsem, dev):
        return pltpu.make_async_remote_copy(
            src_ref=src, dst_ref=dst, send_sem=ssem, recv_sem=rsem,
            device_id={"ha": dev}, device_id_type=pl.DeviceIdType.MESH,
        )

    loads = [
        pltpu.make_async_copy(src, dst, l_sem.at[k])
        for k, (src, dst) in enumerate(
            (
                (wq_hbm, wq), (wk_hbm, wk), (wu_hbm, wu_turned), (w1_hbm, w1),
                (w2_hbm, w2), (wv_hbm, wv), (wo_hbm, wo),
            )
        )
    ]

    barrier = pltpu.get_barrier_semaphore()

    def greet(dev):
        pl.semaphore_signal(
            barrier, inc=1, device_id={"ha": dev}, device_id_type=pl.DeviceIdType.MESH
        )

    greet(partner)
    greet(nxt)
    greet(prv)

    @pl.when(jnp.logical_and(core == 0, low))
    def _():
        greet(2 * chip - 2)
        greet(2 * chip - 1)

    @pl.when(jnp.logical_and(core == 1, high))
    def _():
        greet(2 * chip + 2)
        greet(2 * chip + 3)

    for load in loads:
        load.start()

    pl.semaphore_wait(barrier, 3 + low.astype(jnp.int32) + high.astype(jnp.int32))

    swap = copy(feat.at[other], fb.at[core], e0_s.at[0], e0_r.at[0], partner)
    swap.start()

    def ring_copy(src_slot, slot, row, dev):
        return copy(
            ring.at[src_slot, row], ring.at[slot, row], g_s.at[slot, row], g_r.at[slot, row], dev
        )

    fb[core] = feat[core]
    ring[0, core] = rms(feat[core].astype(F32)).astype(BF16)
    ring_copy(0, 1, core, nxt).start()
    ring_copy(0, chips - 1, core, prv).start()
    copy(feat.at[core], fb.at[other], e0_s.at[0], e0_r.at[0], partner).wait_recv()
    ring[0, other] = rms(fb[other].astype(F32)).astype(BF16)
    ring_copy(0, 1, other, nxt).start()
    ring_copy(0, chips - 1, other, prv).start()

    for parity in range(2):
        pick = (
            lax.broadcasted_iota(jnp.int32, (width, 2 * width), 1)
            == 2 * lax.broadcasted_iota(jnp.int32, (width, 2 * width), 0) + parity
        ).astype(BF16)
        for f in range(2):
            for r in range(2):
                ss[1 + r, parity, f] = dot_t(pick, sc[f, r]).astype(BF16)

    fc_up = copy(fc, fs.at[pl.ds(0, 2), 0], h_s.at[0], h_r.at[0], me + 1)
    fc_down = copy(fc, fs.at[pl.ds(0, 2), 2], h_s.at[1], h_r.at[1], me - 1)
    sc_up = copy(ss.at[2, :, pl.ds(0, 2)], ss.at[0, :, pl.ds(0, 2)], h_s.at[2], h_r.at[2], me + 1)
    sc_down = copy(ss.at[1, :, pl.ds(0, 2)], ss.at[3, :, pl.ds(0, 2)], h_s.at[3], h_r.at[3], me - 1)

    fs[0:2, 1] = fc[...]

    @pl.when(first)
    def _():
        fs[:, 0] = jnp.zeros((4, width, chan), BF16)
        ss[0, :, 0:2] = jnp.zeros((2, 2, width, chan2), BF16)
        bo[0] = jnp.zeros((2, width, chan), BF16)

    @pl.when(last)
    def _():
        fs[:, 2] = jnp.zeros((4, width, chan), BF16)
        ss[3, :, 0:2] = jnp.zeros((2, 2, width, chan2), BF16)
        bo[2] = jnp.zeros((2, width, chan), BF16)

    loads[0].wait()
    loads[1].wait()
    own = ring[0].reshape(2 * width, chan)
    queries = dot(own, wq[...]).astype(BF16)
    queries = (dot_t(queries, wk[...]) * (1.0 / math.sqrt(chan))).astype(BF16)

    def scores_of(slot):
        return dot_t(queries, ring[slot].reshape(2 * width, chan))

    scores = scores_of(0)
    largest = jnp.max(scores, axis=-1, keepdims=True)
    weights = jnp.exp(scores - largest)
    top[...] = largest
    total[...] = jnp.sum(weights, axis=-1, keepdims=True)
    acc[...] = dot(weights.astype(BF16), own)

    def attend(slots):
        parts = [scores_of(slot) for slot in slots]
        before = top[...]
        largest = before
        for part in parts:
            largest = jnp.maximum(largest, jnp.max(part, axis=-1, keepdims=True))
        shrink = jnp.exp(before - largest)
        sums, mixed_in = total[...] * shrink, acc[...] * shrink
        for slot, part in zip(slots, parts):
            weights = jnp.exp(part - largest)
            sums += jnp.sum(weights, axis=-1, keepdims=True)
            mixed_in += dot(weights.astype(BF16), ring[slot].reshape(2 * width, chan))
        top[...] = largest
        total[...] = sums
        acc[...] = mixed_in

    for step in range(1, half):
        for row in (core, other):
            ring_copy(step, step, row, nxt).wait_recv()
            if step + 1 < half:
                ring_copy(step, step + 1, row, nxt).start()
            else:
                pl.when(row == 0)(ring_copy(step, step + 1, 0, nxt).start)
            ring_copy(chips - step, chips - step, row, prv).wait_recv()
            if step + 1 < half:
                ring_copy(chips - step, chips - step - 1, row, prv).start()
            else:
                pl.when(row == 1)(ring_copy(chips - step, chips - step - 1, 1, prv).start)
        attend((step, chips - step))

    pl.when(jnp.logical_not(last))(fc_up.start)
    pl.when(jnp.logical_not(first))(fc_down.start)

    for load in loads[2:]:
        load.wait()

    def first_conv(a, t, c, taps):
        frames = len(t)
        sums = None
        for b in taps:
            rows = fs[a + t[0] : a + t[0] + frames, b].reshape(frames * width, chan)
            term = dot(rows, w1[a, b, c])
            sums = term if sums is None else sums + term
        return sums

    def second_conv(a, t, k, taps, at=0, count=2):
        pairs = (((0, 1), (1, 2)), ((0, 0), (1, 1)), ((1, 0),), ((0, 2),))[k]
        frames = len(t)
        sums = None
        for b in taps:
            for parity, c in pairs:
                rows = ss[at + b : at + b + count, parity, a + t[0] : a + t[0] + frames]
                term = dot(rows.reshape(count * frames * width, chan2), w2[a, b, c])
                sums = term if sums is None else sums + term
        return sums.reshape(count, frames, width, chan2)

    both = (0, 1)
    for c in range(3):
        c1[c] = first_conv(0, both, c, (1,))
        c1[c, :width] += first_conv(1, (0,), c, (1,))
    for k in range(4):
        c2[k] = second_conv(0, both, k, (1,))
        c2[k, 0:1] += second_conv(0, both, k, (2,), 0, 1)
        c2[k, 1:2] += second_conv(0, both, k, (0,), 1, 1)
        c2[k, :, 0:1] += second_conv(1, (0,), k, (1,))
        c2[k, 0:1, 0:1] += second_conv(1, (0,), k, (2,), 0, 1)
        c2[k, 1:2, 0:1] += second_conv(1, (0,), k, (0,), 1, 1)
    for b in range(3):
        for c in range(3):
            wu[b, c] = wu_turned[b, c].T

    ring_copy(half, half, 0, nxt).wait_recv()
    ring_copy(half, half, 1, prv).wait_recv()
    attend((half,))

    attended = dot((acc[...] / total[...]).astype(BF16), wv[...])
    projected = dot(attended.astype(BF16), wo[...])
    mixed = (fb[...].reshape(2 * width, chan).astype(F32) + projected).astype(BF16)
    entering = silu(rms(mixed.astype(F32))).astype(BF16).reshape(2, width, chan)
    mixed = mixed.reshape(2, width, chan)
    mine = 2 + core
    fs[mine, pl.ds(other, 2)] = entering
    mx[0] = mixed[0]
    mx[1] = mixed[1]

    to_partner = copy(
        fs.at[mine, pl.ds(other, 2)], fs.at[mine, pl.ds(core, 2)], e1_s.at[0], e1_r.at[0], partner
    )
    mix_partner = copy(mx.at[other], mx.at[2], e1_s.at[1], e1_r.at[1], partner)
    row_up = copy(
        fs.at[mine, other + 1], fs.at[mine, 0], e1_s.at[2], e1_r.at[2 + core], 2 * chip + 2
    )
    row_down = copy(
        fs.at[mine, other], fs.at[mine, 2], e1_s.at[3], e1_r.at[2 + core], 2 * chip - 1
    )
    pl.when(high)(row_up.start)
    pl.when(low)(row_down.start)
    to_partner.start()
    mix_partner.start()
    pl.when(jnp.logical_not(last))(sc_up.start)
    pl.when(jnp.logical_not(first))(sc_down.start)

    pl.when(jnp.logical_not(first))(fc_up.wait_recv)
    pl.when(jnp.logical_not(last))(fc_down.wait_recv)
    for c in range(3):
        c1[c] += first_conv(0, both, c, (0, 2))
        c1[c, :width] += first_conv(1, (0,), c, (0, 2))

    theirs = 2 + other
    copy(
        fs.at[theirs, pl.ds(core, 2)], fs.at[theirs, pl.ds(other, 2)],
        e1_s.at[0], e1_r.at[0], partner,
    ).wait_recv()
    mix_partner.wait_recv()

    @pl.when(jnp.logical_and(core == 0, low))
    def _():
        for f in range(2):
            copy(
                fs.at[2 + f, 1], fs.at[2 + f, 0], e1_s.at[2], e1_r.at[2 + f], 2 * chip - 2 + f
            ).wait_recv()

    @pl.when(jnp.logical_and(core == 1, high))
    def _():
        for f in range(2):
            copy(
                fs.at[2 + f, 1], fs.at[2 + f, 2], e1_s.at[3], e1_r.at[2 + f], 2 * chip + 2 + f
            ).wait_recv()

    for c in range(3):
        c1[c, width:] += first_conv(1, (1,), c, (0, 1, 2))
    sums = [c1[c] + first_conv(2, both, c, (0, 1, 2)) for c in range(3)]
    block = from_left(sums[0], width) + sums[1] + from_right(sums[2], width)
    block = block.reshape(2, width, chan)
    bo[1, core] = (mx[core].astype(F32) + jnp.where(core == 0, block[0], block[1])).astype(BF16)
    bo[1, other] = (mx[2].astype(F32) + jnp.where(core == 0, block[1], block[0])).astype(BF16)

    bo_up = copy(bo.at[1], bo.at[0], e2_s.at[0], e2_r.at[0], me + 1)
    bo_down = copy(bo.at[1], bo.at[2], e2_s.at[1], e2_r.at[1], me - 1)
    pl.when(jnp.logical_not(last))(bo_up.start)
    pl.when(jnp.logical_not(first))(bo_down.start)

    here = bo[1].reshape(2 * width, chan)
    y = [[dot(here, wu[b, c]) for c in range(3)] for b in range(3)]
    rows = [
        [y[2][c] for c in range(3)],
        [y[1][c] + y[2][c] for c in range(3)],
        [y[0][c] + y[1][c] for c in range(3)],
        [y[0][c] for c in range(3)],
    ]
    pl.when(jnp.logical_not(first))(sc_up.wait_recv)
    pl.when(jnp.logical_not(last))(sc_down.wait_recv)
    for k in range(4):
        c2[k, 0:1] += second_conv(0, both, k, (0,), 0, 1)
        c2[k, 1:2] += second_conv(0, both, k, (2,), 1, 1)
        c2[k, 0:1, 0:1] += second_conv(1, (0,), k, (0,), 0, 1)
        c2[k, 1:2, 0:1] += second_conv(1, (0,), k, (2,), 1, 1)

    pl.when(jnp.logical_not(first))(bo_up.wait_recv)
    pl.when(jnp.logical_not(last))(bo_down.wait_recv)
    above = bo[0].reshape(2 * width, chan)
    below = bo[2].reshape(2 * width, chan)
    for c in range(3):
        near, far = dot(above, wu[0, c]), dot(above, wu[1, c])
        rows[0][c] += near + far
        rows[1][c] += near
        near, far = dot(below, wu[2, c]), dot(below, wu[1, c])
        rows[2][c] += near
        rows[3][c] += near + far
    for u in range(4):
        left, middle, right = rows[u]
        phases = (
            from_left(left, width) + middle + right,
            left + middle + from_right(right, width),
        )
        for parity, value in enumerate(phases):
            value = value.astype(BF16)
            if u in (1, 2):
                up[u - 1, parity] = value.reshape(2, width, chan2)
            entering = silu(rms(value.astype(F32)))
            if u == 0:
                entering = jnp.where(first, 0.0, entering)
            if u == 3:
                entering = jnp.where(last, 0.0, entering)
            ss[u, parity, 2:4] = entering.astype(BF16).reshape(2, width, chan2)

    for k in range(4):
        c2[k, :, 1:2] += second_conv(1, (1,), k, (0, 1, 2))

    def final(k):
        return (c2[k] + second_conv(2, both, k, (0, 1, 2))).reshape(4 * width, chan2)

    even = final(0) + from_left(final(2), width)
    odd = final(1) + from_right(final(3), width)
    even, odd = (
        (up[:, parity].astype(F32) + value.reshape(2, 2, width, chan2)).astype(BF16)
        for parity, value in enumerate((even, odd))
    )
    at = lax.broadcasted_iota(jnp.int32, (2 * width, 2 * width), 0)
    column = lax.broadcasted_iota(jnp.int32, (2 * width, 2 * width), 1)
    place_at = (column == jnp.where(at < width, 2 * at, 2 * at - 2 * width + 1)).astype(BF16)
    for f, out in enumerate((out_0, out_1)):
        for r in range(2):
            pair = jnp.concatenate([even[r, f], odd[r, f]], axis=0)
            out[0, r] = lax.dot_general(
                pair, place_at, (((0,), (0,)), ((), ())), preferred_element_type=F32
            ).astype(BF16)

    swap.wait_send()
    for slot in range(1, chips):
        for row in range(2):
            ring_copy(slot, slot, row, nxt).wait_send()

    @pl.when(jnp.logical_not(last))
    def _():
        fc_up.wait_send()
        sc_up.wait_send()
        bo_up.wait_send()

    @pl.when(jnp.logical_not(first))
    def _():
        fc_down.wait_send()
        sc_down.wait_send()
        bo_down.wait_send()

    pl.when(high)(row_up.wait_send)
    pl.when(low)(row_down.wait_send)
    to_partner.wait_send()
    mix_partner.wait_send()


def per_device(features, first_cache, second_cache, wq, wk, wv, wo, w1, wu, w2):
    n = lax.axis_size("ha")
    width, chan = features.shape[2:]
    chan2 = w2.shape[-1]
    chips = n // 2
    feat = features.reshape(2, width, chan)
    fc = first_cache.reshape(2, width, chan)
    sc = second_cache.transpose(0, 1, 3, 2)
    wu = wu.transpose(0, 1, 3, 2)
    vmem = pl.BlockSpec(memory_space=pltpu.VMEM)
    hbm = pl.BlockSpec(memory_space=pl.ANY)
    dma = pltpu.SemaphoreType.DMA
    out = pl.pallas_call(
        functools.partial(kernel, n),
        out_shape=[jax.ShapeDtypeStruct((1, 2, chan2, 2 * width), BF16)] * 2,
        in_specs=[vmem] * 3 + [hbm] * 7,
        out_specs=[vmem] * 2,
        scratch_shapes=[
            pltpu.VMEM((2, width, chan), BF16),
            pltpu.VMEM((chips, 2, width, chan), BF16),
            pltpu.VMEM((2 * width, chan), F32),
            pltpu.VMEM((2 * width, 1), F32),
            pltpu.VMEM((2 * width, 1), F32),
            pltpu.VMEM((4, 3, width, chan), BF16),
            pltpu.VMEM((3, width, chan), BF16),
            pltpu.VMEM((3, 2, width, chan), BF16),
            pltpu.VMEM((4, 2, 4, width, chan2), BF16),
            pltpu.VMEM((2, 2, 2, width, chan2), BF16),
            pltpu.VMEM((3, 2 * width, chan), F32),
            pltpu.VMEM((4, 2, 2, width, chan2), F32),
            pltpu.VMEM((chan, chan), BF16),
            pltpu.VMEM((chan, chan), BF16),
            pltpu.VMEM((chan, chan), BF16),
            pltpu.VMEM((chan, chan), BF16),
            pltpu.VMEM(w1.shape, BF16),
            pltpu.VMEM((3, 3, chan, chan2), BF16),
            pltpu.VMEM(w2.shape, BF16),
            pltpu.VMEM(wu.shape, BF16),
            dma((7,)),
            dma((1,)),
            dma((1,)),
            dma((chips, 2)),
            dma((chips, 2)),
            dma((4,)),
            dma((4,)),
            dma((4,)),
            dma((4,)),
            dma((2,)),
            dma((2,)),
        ],
        compiler_params=pltpu.CompilerParams(
            collective_id=0, has_side_effects=True, vmem_limit_bytes=56 * 2**20
        ),
        name="decoder_window",
    )(feat, fc, sc, wq, wk, wv, wo, w1, wu, w2)
    return jnp.concatenate(out, axis=0).transpose(0, 1, 3, 2)


def solution(mesh):
    split = P("grp", "ha", None, None)
    return jax.shard_map(
        per_device,
        mesh=mesh,
        in_specs=(split,) * 3 + (P(),) * 7,
        out_specs=split,
        check_vma=False,
    )
```

```python
import functools
import math

import jax
import jax.numpy as jnp
from jax import lax
from jax.experimental import pallas as pl
from jax.experimental.pallas import tpu as pltpu
from jax.sharding import PartitionSpec as P

F32 = jnp.float32
BF16 = jnp.bfloat16


def dot(a, b):
    return jnp.dot(a, b, preferred_element_type=F32)


def dot_t(a, b):
    return lax.dot_general(a, b, (((1,), (1,)), ((), ())), preferred_element_type=F32)


def rms(v):
    return v * lax.rsqrt(jnp.mean(v * v, axis=-1, keepdims=True) + 1e-06)


def silu(v):
    return v * (0.5 + 0.5 * jnp.tanh(0.5 * v))


def from_left(v, width):
    at = lax.broadcasted_iota(jnp.int32, v.shape, 0) % width
    return jnp.where(at == 0, 0.0, pltpu.roll(v, 1, 0))


def from_right(v, width):
    at = lax.broadcasted_iota(jnp.int32, v.shape, 0) % width
    return jnp.where(at == width - 1, 0.0, pltpu.roll(v, v.shape[0] - 1, 0))


def kernel(
    n,
    feat, fc_hbm, sc_hbm, wq_hbm, wk_hbm, wv_hbm, wo_hbm, w1_hbm, wu_hbm, w2_hbm,
    out_0, out_1,
    fb, ring, acc, top, total, fs, mx, bo, ss, up, c1, c2,
    sc, wq, wk, wv, wo, w1, wu, w2, wu_turned,
    l_sem, e0_s, e0_r, g_s, g_r, h_s, h_r, e1_s, e1_r, e2_s, e2_r,
):
    width, chan = feat.shape[1], feat.shape[2]
    chan2 = w2.shape[-1]
    chips = n // 2
    half = chips // 2
    me = lax.axis_index("ha")
    core, chip = me % 2, me // 2
    other = 1 - core
    zz, yy = chip // 2, chip % 2
    place = zz + yy * (2 * half - 1 - 2 * zz)

    def at_place(p):
        side = p // half
        level = p + side * (2 * half - 1 - 2 * p)
        return (level * 2 + side) * 2 + core

    nxt = at_place((place + 1) % chips)
    prv = at_place((place + chips - 1) % chips)
    partner = chip * 2 + other
    first, last = me == 0, me == n - 1
    low, high = chip > 0, chip < chips - 1

    def copy(src, dst, ssem, rsem, dev):
        return pltpu.make_async_remote_copy(
            src_ref=src, dst_ref=dst, send_sem=ssem, recv_sem=rsem,
            device_id={"ha": dev}, device_id_type=pl.DeviceIdType.MESH,
        )

    loads = [
        pltpu.make_async_copy(src, dst, l_sem.at[k])
        for k, (src, dst) in enumerate(
            (
                (sc_hbm, sc), (wq_hbm, wq), (wk_hbm, wk), (fc_hbm, fs.at[pl.ds(0, 2), 1]), (wu_hbm, wu_turned), (w1_hbm, w1),
                (w2_hbm, w2), (wv_hbm, wv), (wo_hbm, wo),
            )
        )
    ]

    barrier = pltpu.get_barrier_semaphore()

    def greet(dev):
        pl.semaphore_signal(
            barrier, inc=1, device_id={"ha": dev}, device_id_type=pl.DeviceIdType.MESH
        )

    greet(partner)
    greet(nxt)
    greet(prv)

    @pl.when(jnp.logical_and(core == 0, low))
    def _():
        greet(2 * chip - 2)
        greet(2 * chip - 1)

    @pl.when(jnp.logical_and(core == 1, high))
    def _():
        greet(2 * chip + 2)
        greet(2 * chip + 3)

    for load in loads:
        load.start()

    pl.semaphore_wait(barrier, 3 + low.astype(jnp.int32) + high.astype(jnp.int32))

    swap = copy(feat.at[other], fb.at[core], e0_s.at[0], e0_r.at[0], partner)
    swap.start()

    def ring_copy(src_slot, slot, row, dev):
        return copy(
            ring.at[src_slot, row], ring.at[slot, row], g_s.at[slot, row], g_r.at[slot, row], dev
        )

    fb[core] = feat[core]
    ring[0, core] = rms(feat[core].astype(F32)).astype(BF16)
    ring_copy(0, 1, core, nxt).start()
    ring_copy(0, chips - 1, core, prv).start()
    copy(feat.at[core], fb.at[other], e0_s.at[0], e0_r.at[0], partner).wait_recv()
    ring[0, other] = rms(fb[other].astype(F32)).astype(BF16)
    ring_copy(0, 1, other, nxt).start()
    ring_copy(0, chips - 1, other, prv).start()

    loads[0].wait()
    for parity in range(2):
        pick = (
            lax.broadcasted_iota(jnp.int32, (width, 2 * width), 1)
            == 2 * lax.broadcasted_iota(jnp.int32, (width, 2 * width), 0) + parity
        ).astype(BF16)
        for f in range(2):
            for r in range(2):
                ss[1 + r, parity, f] = dot_t(pick, sc[f, r]).astype(BF16)

    fc_up = copy(fs.at[pl.ds(0, 2), 1], fs.at[pl.ds(0, 2), 0], h_s.at[0], h_r.at[0], me + 1)
    fc_down = copy(fs.at[pl.ds(0, 2), 1], fs.at[pl.ds(0, 2), 2], h_s.at[1], h_r.at[1], me - 1)
    sc_up = copy(ss.at[2, :, pl.ds(0, 2)], ss.at[0, :, pl.ds(0, 2)], h_s.at[2], h_r.at[2], me + 1)
    sc_down = copy(ss.at[1, :, pl.ds(0, 2)], ss.at[3, :, pl.ds(0, 2)], h_s.at[3], h_r.at[3], me - 1)

    @pl.when(first)
    def _():
        for t in range(4):
            fs[t, 0] = jnp.zeros((width, chan), BF16)
        ss[0, :, 0:2] = jnp.zeros((2, 2, width, chan2), BF16)
        bo[0] = jnp.zeros((2, width, chan), BF16)

    @pl.when(last)
    def _():
        for t in range(4):
            fs[t, 2] = jnp.zeros((width, chan), BF16)
        ss[3, :, 0:2] = jnp.zeros((2, 2, width, chan2), BF16)
        bo[2] = jnp.zeros((2, width, chan), BF16)

    loads[1].wait()
    loads[2].wait()
    own = ring[0].reshape(2 * width, chan)
    queries = dot(own, wq[...]).astype(BF16)
    queries = (dot_t(queries, wk[...]) * (1.0 / math.sqrt(chan))).astype(BF16)

    def scores_of(slot):
        return dot_t(queries, ring[slot].reshape(2 * width, chan))

    scores = scores_of(0)
    largest = jnp.max(scores, axis=-1, keepdims=True)
    weights = jnp.exp(scores - largest)
    top[...] = largest
    total[...] = jnp.sum(weights, axis=-1, keepdims=True)
    acc[...] = dot(weights.astype(BF16), own)

    def attend(slots):
        parts = [scores_of(slot) for slot in slots]
        before = top[...]
        largest = before
        for part in parts:
            largest = jnp.maximum(largest, jnp.max(part, axis=-1, keepdims=True))
        shrink = jnp.exp(before - largest)
        sums, mixed_in = total[...] * shrink, acc[...] * shrink
        for slot, part in zip(slots, parts):
            weights = jnp.exp(part - largest)
            sums += jnp.sum(weights, axis=-1, keepdims=True)
            mixed_in += dot(weights.astype(BF16), ring[slot].reshape(2 * width, chan))
        top[...] = largest
        total[...] = sums
        acc[...] = mixed_in

    def first_conv(a, t, c, taps):
        frames = len(t)
        sums = None
        for b in taps:
            rows = fs[a + t[0] : a + t[0] + frames, b].reshape(frames * width, chan)
            term = dot(rows, w1[a, b, c])
            sums = term if sums is None else sums + term
        return sums

    def second_conv(a, t, k, taps, at=0, count=2):
        pairs = (((0, 1), (1, 2)), ((0, 0), (1, 1)), ((1, 0),), ((0, 2),))[k]
        frames = len(t)
        sums = None
        for b in taps:
            for parity, c in pairs:
                rows = ss[at + b : at + b + count, parity, a + t[0] : a + t[0] + frames]
                term = dot(rows.reshape(count * frames * width, chan2), w2[a, b, c])
                sums = term if sums is None else sums + term
        return sums.reshape(count, frames, width, chan2)

    both = (0, 1)

    def early(step):
        if step == 1:
            for load in loads[3:]:
                load.wait()
            for b in range(3):
                for c in range(3):
                    wu[b, c] = wu_turned[b, c].T
            for c in range(3):
                c1[c] = first_conv(0, both, c, (1,))
                c1[c, :width] += first_conv(1, (0,), c, (1,))
        for k in {2: (0, 1), 3: (2, 3)}.get(min(step, 4), ()):
            c2[k] = second_conv(0, both, k, (1,))
            c2[k, 0:1] += second_conv(0, both, k, (2,), 0, 1)
            c2[k, 1:2] += second_conv(0, both, k, (0,), 1, 1)
            c2[k, :, 0:1] += second_conv(1, (0,), k, (1,))
            c2[k, 0:1, 0:1] += second_conv(1, (0,), k, (2,), 0, 1)
            c2[k, 1:2, 0:1] += second_conv(1, (0,), k, (0,), 1, 1)

    for step in range(1, half):
        for row in (core, other):
            ring_copy(step, step, row, nxt).wait_recv()
            if step + 1 < half:
                ring_copy(step, step + 1, row, nxt).start()
            else:
                pl.when(row == 0)(ring_copy(step, step + 1, 0, nxt).start)
            ring_copy(chips - step, chips - step, row, prv).wait_recv()
            if step + 1 < half:
                ring_copy(chips - step, chips - step - 1, row, prv).start()
            else:
                pl.when(row == 1)(ring_copy(chips - step, chips - step - 1, 1, prv).start)
        if step + 1 == half:
            pl.when(jnp.logical_not(last))(fc_up.start)
            pl.when(jnp.logical_not(first))(fc_down.start)
        attend((step, chips - step))
        early(step)

    ring_copy(half, half, 0, nxt).wait_recv()
    ring_copy(half, half, 1, prv).wait_recv()
    attend((half,))

    attended = dot((acc[...] / total[...]).astype(BF16), wv[...])
    projected = dot(attended.astype(BF16), wo[...])
    mixed = (fb[...].reshape(2 * width, chan).astype(F32) + projected).astype(BF16)
    entering = silu(rms(mixed.astype(F32))).astype(BF16).reshape(2, width, chan)
    mixed = mixed.reshape(2, width, chan)
    mine = 2 + core
    fs[mine, pl.ds(other, 2)] = entering
    mx[0] = mixed[0]
    mx[1] = mixed[1]

    to_partner = copy(
        fs.at[mine, pl.ds(other, 2)], fs.at[mine, pl.ds(core, 2)], e1_s.at[0], e1_r.at[0], partner
    )
    mix_partner = copy(mx.at[other], mx.at[2], e1_s.at[1], e1_r.at[1], partner)
    row_up = copy(
        fs.at[mine, other + 1], fs.at[mine, 0], e1_s.at[2], e1_r.at[2 + core], 2 * chip + 2
    )
    row_down = copy(
        fs.at[mine, other], fs.at[mine, 2], e1_s.at[3], e1_r.at[2 + core], 2 * chip - 1
    )
    pl.when(high)(row_up.start)
    pl.when(low)(row_down.start)
    to_partner.start()
    mix_partner.start()
    pl.when(jnp.logical_not(last))(sc_up.start)
    pl.when(jnp.logical_not(first))(sc_down.start)

    pl.when(jnp.logical_not(first))(fc_up.wait_recv)
    pl.when(jnp.logical_not(last))(fc_down.wait_recv)
    for c in range(3):
        c1[c] += first_conv(0, both, c, (0, 2))
        c1[c, :width] += first_conv(1, (0,), c, (0, 2))

    theirs = 2 + other
    copy(
        fs.at[theirs, pl.ds(core, 2)], fs.at[theirs, pl.ds(other, 2)],
        e1_s.at[0], e1_r.at[0], partner,
    ).wait_recv()
    mix_partner.wait_recv()

    @pl.when(jnp.logical_and(core == 0, low))
    def _():
        for f in range(2):
            copy(
                fs.at[2 + f, 1], fs.at[2 + f, 0], e1_s.at[2], e1_r.at[2 + f], 2 * chip - 2 + f
            ).wait_recv()

    @pl.when(jnp.logical_and(core == 1, high))
    def _():
        for f in range(2):
            copy(
                fs.at[2 + f, 1], fs.at[2 + f, 2], e1_s.at[3], e1_r.at[2 + f], 2 * chip + 2 + f
            ).wait_recv()


    for c in range(3):
        c1[c, width:] += first_conv(1, (1,), c, (0, 1, 2))
    sums = [c1[c] + first_conv(2, both, c, (0, 1, 2)) for c in range(3)]
    block = from_left(sums[0], width) + sums[1] + from_right(sums[2], width)
    block = block.reshape(2, width, chan)
    bo[1, core] = (mx[core].astype(F32) + jnp.where(core == 0, block[0], block[1])).astype(BF16)
    bo[1, other] = (mx[2].astype(F32) + jnp.where(core == 0, block[1], block[0])).astype(BF16)

    bo_up = copy(bo.at[1], bo.at[0], e2_s.at[0], e2_r.at[0], me + 1)
    bo_down = copy(bo.at[1], bo.at[2], e2_s.at[1], e2_r.at[1], me - 1)
    pl.when(jnp.logical_not(last))(bo_up.start)
    pl.when(jnp.logical_not(first))(bo_down.start)

    here = bo[1].reshape(2 * width, chan)
    y = [[dot(here, wu[b, c]) for c in range(3)] for b in range(3)]
    rows = [
        [y[2][c] for c in range(3)],
        [y[1][c] + y[2][c] for c in range(3)],
        [y[0][c] + y[1][c] for c in range(3)],
        [y[0][c] for c in range(3)],
    ]
    pl.when(jnp.logical_not(first))(sc_up.wait_recv)
    pl.when(jnp.logical_not(last))(sc_down.wait_recv)
    for k in range(4):
        c2[k, 0:1] += second_conv(0, both, k, (0,), 0, 1)
        c2[k, 1:2] += second_conv(0, both, k, (2,), 1, 1)
        c2[k, 0:1, 0:1] += second_conv(1, (0,), k, (0,), 0, 1)
        c2[k, 1:2, 0:1] += second_conv(1, (0,), k, (2,), 1, 1)

    pl.when(jnp.logical_not(first))(bo_up.wait_recv)
    pl.when(jnp.logical_not(last))(bo_down.wait_recv)
    above = bo[0].reshape(2 * width, chan)
    below = bo[2].reshape(2 * width, chan)
    for c in range(3):
        near, far = dot(above, wu[0, c]), dot(above, wu[1, c])
        rows[0][c] += near + far
        rows[1][c] += near
        near, far = dot(below, wu[2, c]), dot(below, wu[1, c])
        rows[2][c] += near
        rows[3][c] += near + far
    for u in range(4):
        left, middle, right = rows[u]
        phases = (
            from_left(left, width) + middle + right,
            left + middle + from_right(right, width),
        )
        for parity, value in enumerate(phases):
            value = value.astype(BF16)
            if u in (1, 2):
                up[u - 1, parity] = value.reshape(2, width, chan2)
            entering = silu(rms(value.astype(F32)))
            if u == 0:
                entering = jnp.where(first, 0.0, entering)
            if u == 3:
                entering = jnp.where(last, 0.0, entering)
            ss[u, parity, 2:4] = entering.astype(BF16).reshape(2, width, chan2)

    for k in range(4):
        c2[k, :, 1:2] += second_conv(1, (1,), k, (0, 1, 2))

    def final(k):
        return (c2[k] + second_conv(2, both, k, (0, 1, 2))).reshape(4 * width, chan2)

    even = final(0) + from_left(final(2), width)
    odd = final(1) + from_right(final(3), width)
    even, odd = (
        (up[:, parity].astype(F32) + value.reshape(2, 2, width, chan2)).astype(BF16)
        for parity, value in enumerate((even, odd))
    )
    at = lax.broadcasted_iota(jnp.int32, (2 * width, 2 * width), 0)
    column = lax.broadcasted_iota(jnp.int32, (2 * width, 2 * width), 1)
    place_at = (column == jnp.where(at < width, 2 * at, 2 * at - 2 * width + 1)).astype(BF16)
    for f, out in enumerate((out_0, out_1)):
        for r in range(2):
            pair = jnp.concatenate([even[r, f], odd[r, f]], axis=0)
            out[0, r] = lax.dot_general(
                pair, place_at, (((0,), (0,)), ((), ())), preferred_element_type=F32
            ).astype(BF16)

    swap.wait_send()
    for slot in range(1, chips):
        for row in range(2):
            ring_copy(slot, slot, row, nxt).wait_send()

    @pl.when(jnp.logical_not(last))
    def _():
        fc_up.wait_send()
        sc_up.wait_send()
        bo_up.wait_send()

    @pl.when(jnp.logical_not(first))
    def _():
        fc_down.wait_send()
        sc_down.wait_send()
        bo_down.wait_send()

    pl.when(high)(row_up.wait_send)
    pl.when(low)(row_down.wait_send)
    to_partner.wait_send()
    mix_partner.wait_send()


def per_device(features, first_cache, second_cache, wq, wk, wv, wo, w1, wu, w2):
    n = lax.axis_size("ha")
    width, chan = features.shape[2:]
    chan2 = w2.shape[-1]
    chips = n // 2
    feat = features.reshape(2, width, chan)
    fc = first_cache.reshape(2, width, chan)
    sc = second_cache.transpose(0, 1, 3, 2)
    wu = wu.transpose(0, 1, 3, 2)
    vmem = pl.BlockSpec(memory_space=pltpu.VMEM)
    hbm = pl.BlockSpec(memory_space=pl.ANY)
    dma = pltpu.SemaphoreType.DMA
    out = pl.pallas_call(
        functools.partial(kernel, n),
        out_shape=[jax.ShapeDtypeStruct((1, 2, chan2, 2 * width), BF16)] * 2,
        in_specs=[vmem] + [hbm] * 9,
        out_specs=[vmem] * 2,
        scratch_shapes=[
            pltpu.VMEM((2, width, chan), BF16),
            pltpu.VMEM((chips, 2, width, chan), BF16),
            pltpu.VMEM((2 * width, chan), F32),
            pltpu.VMEM((2 * width, 1), F32),
            pltpu.VMEM((2 * width, 1), F32),
            pltpu.VMEM((4, 3, width, chan), BF16),
            pltpu.VMEM((3, width, chan), BF16),
            pltpu.VMEM((3, 2, width, chan), BF16),
            pltpu.VMEM((4, 2, 4, width, chan2), BF16),
            pltpu.VMEM((2, 2, 2, width, chan2), BF16),
            pltpu.VMEM((3, 2 * width, chan), F32),
            pltpu.VMEM((4, 2, 2, width, chan2), F32),
            pltpu.VMEM(sc.shape, BF16),
            pltpu.VMEM((chan, chan), BF16),
            pltpu.VMEM((chan, chan), BF16),
            pltpu.VMEM((chan, chan), BF16),
            pltpu.VMEM((chan, chan), BF16),
            pltpu.VMEM(w1.shape, BF16),
            pltpu.VMEM((3, 3, chan, chan2), BF16),
            pltpu.VMEM(w2.shape, BF16),
            pltpu.VMEM(wu.shape, BF16),
            dma((9,)),
            dma((1,)),
            dma((1,)),
            dma((chips, 2)),
            dma((chips, 2)),
            dma((4,)),
            dma((4,)),
            dma((4,)),
            dma((4,)),
            dma((2,)),
            dma((2,)),
        ],
        compiler_params=pltpu.CompilerParams(
            collective_id=0, has_side_effects=True, vmem_limit_bytes=56 * 2**20
        ),
        name="decoder_window",
    )(feat, fc, sc, wq, wk, wv, wo, w1, wu, w2)
    return jnp.concatenate(out, axis=0).transpose(0, 1, 3, 2)


def solution(mesh):
    split = P("grp", "ha", None, None)
    return jax.shard_map(
        per_device,
        mesh=mesh,
        in_specs=(split,) * 3 + (P(),) * 7,
        out_specs=split,
        check_vma=False,
    )
```
